512 devices in a mesh: row: 16 (over x, y_lo, core), col: 32 (over y_hi, z).
Axes of the slice: x: 4, y: 8 (y_hi: 4, y_lo: 2; y = y_hi * 2 + y_lo), z: 8, core: 2. Of those that a mesh axis runs over, the one named last changes fastest.
Arguments:
- vectors: float32 [8, 65536], P(None, ('row', 'col')), may hold values from -6 to 6
- diagonal: float32 [65536], P(('row', 'col'))
- blocks: float32 [16, 32, 8, 128, 128], P('row', 'col'), may hold values from -0.125 to 0.125
- block_rows: int32 [16, 32, 8], P('row', 'col'), may hold values from 0 to 31
- block_cols: int32 [16, 32, 8], P('row', 'col'), may hold values from 0 to 15
- counts: int32 [16, 32], P('row', 'col'), may hold values from 4 to 8, as said below
Outputs:
- eigvecs: float32 [8, 65536], P(None, ('row', 'col'))
- factor: float32 [8, 8], replicated
The draws below stay inside these ranges and needn't reach their ends.
Inputs may be any that keep to these rules, and one draw needn't show every extreme that they name: `counts`: every device has at least half of its 8 slots live, and some device has all 8 live.
All inputs are finite; a program needn't handle non-finite values.
Results may differ from the reference program's by a relative error of at most 0.0001.
Values sent between devices are 32-bit elements; how exact they have to be, the bound alone decides.
A program may use at most 64 MiB of HBM per device.

```python
import jax
import jax.numpy as jnp
from jax import lax

BS = 128
K = 8
ITERS = 4
BL = 8
NS = 65536
N_ROW = 16
N_COL = 32


def draw_diagonal(key, part):
    place = jnp.arange(NS).astype(jnp.float32) / NS
    rough = jnp.exp(jax.random.uniform(key, (NS,), jnp.float32, 0.0, jnp.log(3.0)))
    return rough * (1.0 + 2.0 * place)


def draw_counts(key, part):
    first = jax.random.fold_in(key, 11)
    second = jax.random.fold_in(key, 23)
    values = jax.random.randint(first, (N_ROW * N_COL,), BL // 2, BL + 1)
    spot = jax.random.randint(second, (), 0, N_ROW * N_COL)
    values = jnp.where(jnp.arange(N_ROW * N_COL) == spot, BL, values)
    return values.reshape(N_ROW, N_COL).astype(jnp.int32)


def plant(values, own_key, least, top_value):
    spot = [jax.random.randint(jax.random.fold_in(own_key, axis), (), 0, length) for axis, length in enumerate(values.shape)]
    main_axis = values.shape.index(max(values.shape))
    next_to = spot[:main_axis] + [(spot[main_axis] + 1) % values.shape[main_axis]] + spot[main_axis + 1:]
    return values.at[tuple(spot)].set(least).at[tuple(next_to)].set(top_value)


def block_levels(key, shape, split, low, top_value):
    gain = 1.0
    for position, parts in split:
        heights = jax.random.uniform(jax.random.fold_in(jax.random.fold_in(key, 6), position), (parts,), jnp.float32, low / len(split), top_value / len(split))
        gain = gain * jnp.repeat(jnp.exp(heights), shape[position] // parts).reshape((-1,) + (1,) * (len(shape) - 1 - position))
    return gain


def normal_values(rng, dims, width, bound, cuts=(), kind=jnp.bfloat16):
    entries = width * jax.random.normal(rng, dims, jnp.float32)
    if cuts:
        entries = entries * block_levels(rng, dims, cuts, -0.22, 0.18)
    return jnp.clip(entries, -bound, bound).astype(kind)


def setup_inputs(seed: int = 0) -> dict:
    seeds = jax.random.split(jax.random.key(seed), 7)
    return {
        "vectors": normal_values(seeds[0], (K, NS), 1.0, 6.0, ((1, 512),), jnp.float32),
        "diagonal": draw_diagonal(jax.random.fold_in(seeds[6], 71), 0),
        "blocks": normal_values(seeds[2], (N_ROW, N_COL, BL, BS, BS), (2 * BL * BS) ** -0.5, 0.125, ((0, 16), (1, 32)), jnp.float32),
        "block_rows": plant(jax.random.randint(seeds[3], (N_ROW, N_COL, BL), 0, N_COL), jax.random.fold_in(seeds[3], 1), 0, N_COL - 1).astype(jnp.int32),
        "block_cols": plant(jax.random.randint(seeds[4], (N_ROW, N_COL, BL), 0, N_ROW), jax.random.fold_in(seeds[4], 1), 0, N_ROW - 1).astype(jnp.int32),
        "counts": draw_counts(jax.random.fold_in(seeds[6], 71), 0),
    }


def reference(vectors, diagonal, blocks, block_rows, block_cols, counts):
    high = lax.Precision.HIGHEST
    nvec = vectors.shape[0]
    slots = jnp.arange(BL).astype(jnp.int32)
    live = (slots[None, None, :] < counts[:, :, None]).astype(jnp.float32)
    row_select = (block_rows[..., None] == jnp.arange(N_COL).astype(jnp.int32)).astype(jnp.float32) * live[..., None]
    col_select = (block_cols[..., None] == jnp.arange(N_ROW).astype(jnp.int32)).astype(jnp.float32) * live[..., None]
    blocks_f = blocks.astype(jnp.float32)
    current = vectors
    lower = jnp.eye(nvec, dtype=jnp.float32)
    for step in range(ITERS):
        grid_x = current.reshape(nvec, N_ROW, N_COL, BS)
        col_input = jnp.einsum('rcbq,kqcj->krcbj', col_select, grid_x, precision=high)
        direct = jnp.einsum('rcbij,krcbj->krcbi', blocks_f, col_input, precision=high)
        direct_sum = jnp.einsum('rcbq,krcbi->krqi', row_select, direct, precision=high).reshape(nvec, NS)
        row_input = jnp.einsum('rcbq,krqi->krcbi', row_select, grid_x, precision=high)
        transposed = jnp.einsum('rcbij,krcbi->krcbj', blocks_f, row_input, precision=high)
        transposed_sum = jnp.einsum('rcbq,krcbj->kqcj', col_select, transposed, precision=high).reshape(nvec, NS)
        images = diagonal[None, :] * current + direct_sum + transposed_sum
        gram = jnp.dot(images.astype(jnp.float32), images.T.astype(jnp.float32), precision=high, preferred_element_type=jnp.float32)
        lower = jnp.linalg.cholesky(gram)
        current = lax.linalg.triangular_solve(lower, images, left_side=True, lower=True)
    return (current, lower)
```

```python
import functools

import jax
import jax.numpy as jnp
from jax import lax
from jax.experimental import pallas as pl
from jax.experimental.pallas import tpu as pltpu
from jax.sharding import PartitionSpec as P

ITERS = 4
MESH = pl.DeviceIdType.MESH
F32 = jnp.float32
BF16 = jnp.bfloat16


def split_rows(x):
    hi = x.astype(BF16).astype(F32)
    return jnp.concatenate([hi, x - hi], axis=0).astype(BF16)


def product(both, pair):
    out = jnp.dot(both, pair, preferred_element_type=F32)
    k = both.shape[0] // 2
    n = pair.shape[1] // 2
    return (out[:k, :n] + (out[k:, :n] + out[:k, n:])) + out[k:, n:]


def gram_of(wide):
    both = split_rows(wide)
    k = wide.shape[0]
    dims = (((1,), (1,)), ((), ()))
    high = both[:k]
    low = both[k:]
    a = lax.dot_general(both, high, dims, preferred_element_type=F32)
    b = lax.dot_general(both, low, dims, preferred_element_type=F32)
    return (a[:k] + (a[k:] + b[:k])) + b[k:]


def factor(gram):
    k, lanes = gram.shape
    row = lax.broadcasted_iota(jnp.int32, (k, lanes), 0)
    lane = lax.broadcasted_iota(jnp.int32, (k, lanes), 1)
    a = jnp.where(lane < k, gram, jnp.where(lane - k == row, 1.0, 0.0))
    lower = jnp.zeros((k, lanes), F32)
    scale = jnp.zeros((k, lanes), F32)
    for j in range(k):
        col = jnp.broadcast_to(a[:, j : j + 1], (k, lanes))
        pivot_row = jnp.broadcast_to(a[j : j + 1, :], (k, lanes))
        pivot = jnp.broadcast_to(col[j : j + 1, :], (k, lanes))
        root = lax.rsqrt(pivot)
        a = a - jnp.where(row > j, col * (1.0 / pivot), 0.0) * pivot_row
        lower = jnp.where((lane == j) & (row >= j), col * root, lower)
        scale = jnp.where(row == j, root, scale)
    return lower, a * scale


def columns_of(inverse):
    k, lanes = inverse.shape
    return [jnp.broadcast_to(inverse[:, k + j : k + j + 1], (k, lanes)) for j in range(k)]


def apply(columns, values):
    k, lanes = values.shape
    terms = [columns[j] * jnp.broadcast_to(values[j : j + 1, :], (k, lanes)) for j in range(k)]
    while len(terms) > 1:
        terms = [a + b for a, b in zip(terms[::2], terms[1::2])]
    return terms[0]


def tree_sum(values):
    values = list(values)
    while len(values) > 1:
        pairs = [a + b for a, b in zip(values[::2], values[1::2])]
        if len(values) % 2:
            pairs.append(values[-1])
        values = pairs
    return values[0]


def kernel(
    n_row, n_col, n_hi, n_lo,
    vec, diag, blocks, rows_s, cols_s, count_s,
    out_x, out_l,
    s_in, s_nn, s_tt,
    x_send, d_send, t_send, ga_send, gb_send,
    rg, cg, cs, rs, ga, gb,
    in_sem,
    rg_ss, cg_ss, cs_ss, rs_ss, ga_ss, gb_ss,
    rg_rs, cg_rs, cs_rs, rs_rs, ga_rs, gb_rs,
    fr, fc, f_send, f_ss, f_rs,
    row_in, col_in,
):
    slots = rows_s.shape[0]
    k, width = vec.shape
    r = lax.axis_index("row")
    c = lax.axis_index("col")
    hi = c // n_lo
    lo = lax.rem(c, n_lo)

    load = pltpu.make_async_copy(blocks, s_in, in_sem)
    load.start()

    barrier = pltpu.get_barrier_semaphore()

    def greet_row(i, _):
        pl.semaphore_signal(barrier, inc=1, device_id=(lax.rem(r + i, n_row), c), device_id_type=MESH)
        return 0

    def greet_col(i, _):
        pl.semaphore_signal(barrier, inc=1, device_id=(r, lax.rem(c + i, n_col)), device_id_type=MESH)
        return 0

    lax.fori_loop(1, n_row, greet_row, 0)
    lax.fori_loop(1, n_col, greet_col, 0)

    load.wait()
    live = count_s[0]
    for b in range(slots):
        keep = jnp.where(b < live, 1.0, 0.0).astype(F32)
        s = s_in[b] * keep
        t = jnp.transpose(s)
        s_hi = s.astype(BF16)
        s_nn[b, :, :width] = s_hi
        s_nn[b, :, width:] = (s - s_hi.astype(F32)).astype(BF16)
        t_hi = t.astype(BF16)
        s_tt[b, :, :width] = t_hi
        s_tt[b, :, width:] = (t - t_hi.astype(F32)).astype(BF16)

    x_send[...] = vec[...]
    ga_send[...] = jnp.zeros_like(ga_send)
    f_send[...] = jnp.zeros_like(f_send)
    pl.semaphore_wait(barrier, n_row + n_col - 2)

    def to_row(i, src, dst, send_sem, recv_sem):
        pltpu.make_async_remote_copy(
            src_ref=src, dst_ref=dst, send_sem=send_sem, recv_sem=recv_sem,
            device_id=(lax.rem(r + i, n_row), c), device_id_type=MESH,
        ).start()

    def to_col(peer, src, dst, send_sem, recv_sem):
        pltpu.make_async_remote_copy(
            src_ref=src, dst_ref=dst, send_sem=send_sem, recv_sem=recv_sem,
            device_id=(r, peer), device_id_type=MESH,
        ).start()

    def drain(pieces, sem):
        pltpu.make_async_copy(pieces, pieces, sem).wait()

    def step(t, _):
        p = lax.rem(t, 2)
        current = x_send[...]

        def gather_row(i, _):
            to_row(i, x_send, rg.at[p, r], rg_ss, rg_rs.at[p])
            return 0

        def gather_col(i, _):
            to_col(lax.rem(c + i, n_col), x_send, cg.at[p, c], cg_ss, cg_rs.at[p])
            return 0

        lax.fori_loop(1, n_row, gather_row, 0)
        lax.fori_loop(1, n_col, gather_col, 0)
        rg[p, r] = current
        cg[p, c] = current

        drain(rg.at[p, pl.ds(0, n_row - 1)], rg_rs.at[p])
        pieces = [rg[p, q] for q in range(n_row)]
        for q in range(n_row):
            row_in[q] = pieces[q]
        ga_send[:, :k] = gram_of(jnp.concatenate(pieces, axis=1))

        def gram_hi(i, _):
            to_col(lax.rem(hi + i, n_hi) * n_lo + lo, ga_send, ga.at[p, hi], ga_ss, ga_rs.at[p])
            return 0

        lax.fori_loop(1, n_hi, gram_hi, 0)
        ga[p, hi] = ga_send[...]

        direct = [product(split_rows(row_in[cols_s[b]]), s_tt[b]) for b in range(slots)]
        where_row = [rows_s[b] for b in range(slots)]

        def scatter_col(i, _):
            q = lax.rem(c + i, n_col)
            d_send[q] = tree_sum(jnp.where(where_row[b] == q, direct[b], 0.0) for b in range(slots))
            to_col(q, d_send.at[q], cs.at[p, c], cs_ss, cs_rs.at[p])
            return 0

        lax.fori_loop(1, n_col, scatter_col, 0)
        cs[p, c] = tree_sum(jnp.where(where_row[b] == c, direct[b], 0.0) for b in range(slots))

        drain(ga.at[p, pl.ds(0, n_hi - 1)], ga_rs.at[p])
        gb_send[...] = tree_sum(ga[p, i] for i in range(n_hi))

        def gram_lo(i, _):
            to_col(hi * n_lo + lax.rem(lo + i, n_lo), gb_send, gb.at[p, lo], gb_ss, gb_rs.at[p])
            return 0

        lax.fori_loop(1, n_lo, gram_lo, 0)
        gb[p, lo] = gb_send[...]

        drain(cg.at[p, pl.ds(0, n_col - 1)], cg_rs.at[p])
        for q in range(n_col):
            col_in[q] = cg[p, q]
        trans = [product(split_rows(col_in[rows_s[b]]), s_nn[b]) for b in range(slots)]
        where_col = [cols_s[b] for b in range(slots)]

        def scatter_row(i, _):
            q = lax.rem(r + i, n_row)
            t_send[q] = tree_sum(jnp.where(where_col[b] == q, trans[b], 0.0) for b in range(slots))
            to_row(i, t_send.at[q], rs.at[p, r], rs_ss, rs_rs.at[p])
            return 0

        lax.fori_loop(1, n_row, scatter_row, 0)
        rs[p, r] = tree_sum(jnp.where(where_col[b] == r, trans[b], 0.0) for b in range(slots))

        drain(gb.at[p, pl.ds(0, n_lo - 1)], gb_rs.at[p])
        gram = tree_sum(gb[p, i] for i in range(n_lo))
        row = lax.broadcasted_iota(jnp.int32, gram.shape, 0)
        lane = lax.broadcasted_iota(jnp.int32, gram.shape, 1)
        gram = jnp.where(t == 0, jnp.where(row == lane, 1.0, 0.0), gram)
        columns = columns_of(factor(gram)[1])

        drain(rg.at[p, pl.ds(0, n_row - 1)], rg_ss)
        drain(cg.at[p, pl.ds(0, n_col - 1)], cg_ss)
        drain(ga.at[p, pl.ds(0, n_hi - 1)], ga_ss)
        drain(gb.at[p, pl.ds(0, n_lo - 1)], gb_ss)

        drain(cs.at[p, pl.ds(0, n_col - 1)], cs_rs.at[p])
        direct_sum = tree_sum(cs[p, i] for i in range(n_col))
        drain(rs.at[p, pl.ds(0, n_row - 1)], rs_rs.at[p])
        trans_sum = tree_sum(rs[p, i] for i in range(n_row))
        images = diag[...] * current + direct_sum + trans_sum
        x_send[...] = apply(columns, images)
        drain(cs.at[p, pl.ds(0, n_col - 1)], cs_ss)
        drain(rs.at[p, pl.ds(0, n_row - 1)], rs_ss)
        return 0

    lax.fori_loop(0, ITERS, step, 0)

    images = x_send[...]
    f_send[0, :, :k] = gram_of(images)

    def last_row(i, _):
        to_row(i, f_send.at[0], fr.at[r], f_ss.at[0], f_rs.at[0])
        return 0

    lax.fori_loop(1, n_row, last_row, 0)
    fr[r] = f_send[0]
    drain(fr.at[pl.ds(0, n_row - 1)], f_rs.at[0])
    f_send[1] = tree_sum(fr[i] for i in range(n_row))

    def last_col(i, _):
        to_col(lax.rem(c + i, n_col), f_send.at[1], fc.at[c], f_ss.at[1], f_rs.at[1])
        return 0

    lax.fori_loop(1, n_col, last_col, 0)
    fc[c] = f_send[1]
    drain(fc.at[pl.ds(0, n_col - 1)], f_rs.at[1])
    lower, inverse = factor(tree_sum(fc[i] for i in range(n_col)))
    out_x[...] = apply(columns_of(inverse), images)
    out_l[...] = lower[:, :k]
    drain(fr.at[pl.ds(0, n_row - 1)], f_ss.at[0])
    drain(fc.at[pl.ds(0, n_col - 1)], f_ss.at[1])


def solution(mesh):
    n_row, n_col = mesh.shape["row"], mesh.shape["col"]
    n_hi = 4 if n_col % 4 == 0 and n_col > 4 else 2
    n_lo = n_col // n_hi

    def shards(vectors, diagonal, blocks, block_rows, block_cols, counts):
        k, width = vectors.shape
        slots = blocks.shape[2]
        piece = (k, width)
        vmem = pl.BlockSpec(memory_space=pltpu.VMEM)
        smem = pl.BlockSpec(memory_space=pltpu.SMEM)
        dma = pltpu.SemaphoreType.DMA
        return pl.pallas_call(
            functools.partial(kernel, n_row, n_col, n_hi, n_lo),
            out_shape=(jax.ShapeDtypeStruct(piece, F32), jax.ShapeDtypeStruct((k, k), F32)),
            in_specs=[vmem, vmem, pl.BlockSpec(memory_space=pl.ANY), smem, smem, smem],
            out_specs=(vmem, vmem),
            scratch_shapes=[
                pltpu.VMEM((slots, width, width), F32),
                pltpu.VMEM((slots, width, 2 * width), BF16),
                pltpu.VMEM((slots, width, 2 * width), BF16),
                pltpu.VMEM(piece, F32),
                pltpu.VMEM((n_col,) + piece, F32),
                pltpu.VMEM((n_row,) + piece, F32),
                pltpu.VMEM(piece, F32),
                pltpu.VMEM(piece, F32),
                pltpu.VMEM((2, n_row) + piece, F32),
                pltpu.VMEM((2, n_col) + piece, F32),
                pltpu.VMEM((2, n_col) + piece, F32),
                pltpu.VMEM((2, n_row) + piece, F32),
                pltpu.VMEM((2, n_hi) + piece, F32),
                pltpu.VMEM((2, n_lo) + piece, F32),
                dma,
                dma, dma, dma, dma, dma, dma,
                dma((2,)), dma((2,)), dma((2,)), dma((2,)), dma((2,)), dma((2,)),
                pltpu.VMEM((n_row,) + piece, F32),
                pltpu.VMEM((n_col,) + piece, F32),
                pltpu.VMEM((2,) + piece, F32),
                dma((2,)),
                dma((2,)),
                pltpu.VMEM((n_row,) + piece, F32),
                pltpu.VMEM((n_col,) + piece, F32),
            ],
            compiler_params=pltpu.CompilerParams(
                collective_id=0, has_side_effects=True, vmem_limit_bytes=24 * 1024 * 1024
            ),
        )(
            vectors, diagonal.reshape(1, width), blocks.reshape(slots, width, width),
            block_rows.reshape(slots), block_cols.reshape(slots), counts.reshape(1),
        )

    return jax.shard_map(
        shards,
        mesh=mesh,
        in_specs=(
            P(None, ("row", "col")),
            P(("row", "col")),
            P("row", "col", None, None, None),
            P("row", "col", None),
            P("row", "col", None),
            P("row", "col"),
        ),
        out_specs=(P(None, ("row", "col")), P()),
        check_vma=False,
    )
```

```python
import functools

import jax
import jax.numpy as jnp
from jax import lax
from jax.experimental import pallas as pl
from jax.experimental.pallas import tpu as pltpu
from jax.sharding import PartitionSpec as P

ITERS = 4
MESH = pl.DeviceIdType.MESH
F32 = jnp.float32
BF16 = jnp.bfloat16


def split_rows(x):
    hi = x.astype(BF16).astype(F32)
    return jnp.concatenate([hi, x - hi], axis=0).astype(BF16)


def product(both, pair):
    out = jnp.dot(both, pair, preferred_element_type=F32)
    k = both.shape[0] // 2
    n = pair.shape[1] // 2
    return (out[:k, :n] + (out[k:, :n] + out[:k, n:])) + out[k:, n:]


def gram_of(wide):
    both = split_rows(wide)
    k = wide.shape[0]
    dims = (((1,), (1,)), ((), ()))
    high = both[:k]
    low = both[k:]
    a = lax.dot_general(both, high, dims, preferred_element_type=F32)
    b = lax.dot_general(both, low, dims, preferred_element_type=F32)
    return (a[:k] + (a[k:] + b[:k])) + b[k:]


def factor(gram):
    k, lanes = gram.shape
    row = lax.broadcasted_iota(jnp.int32, (k, lanes), 0)
    lane = lax.broadcasted_iota(jnp.int32, (k, lanes), 1)
    a = jnp.where(lane < k, gram, jnp.where(lane - k == row, 1.0, 0.0))
    lower = jnp.zeros((k, lanes), F32)
    scale = jnp.zeros((k, lanes), F32)
    for j in range(k):
        col = jnp.broadcast_to(a[:, j : j + 1], (k, lanes))
        pivot_row = jnp.broadcast_to(a[j : j + 1, :], (k, lanes))
        pivot = jnp.broadcast_to(col[j : j + 1, :], (k, lanes))
        root = lax.rsqrt(pivot)
        a = a - jnp.where(row > j, col * (1.0 / pivot), 0.0) * pivot_row
        lower = jnp.where((lane == j) & (row >= j), col * root, lower)
        scale = jnp.where(row == j, root, scale)
    return lower, a * scale


def columns_of(inverse):
    k, lanes = inverse.shape
    return [jnp.broadcast_to(inverse[:, k + j : k + j + 1], (k, lanes)) for j in range(k)]


def apply(columns, values):
    k, lanes = values.shape
    terms = [columns[j] * jnp.broadcast_to(values[j : j + 1, :], (k, lanes)) for j in range(k)]
    while len(terms) > 1:
        terms = [a + b for a, b in zip(terms[::2], terms[1::2])]
    return terms[0]


def tree_sum(values):
    values = list(values)
    while len(values) > 1:
        pairs = [a + b for a, b in zip(values[::2], values[1::2])]
        if len(values) % 2:
            pairs.append(values[-1])
        values = pairs
    return values[0]


def far_first(n, i):
    return n // 2 + ((i + 1) // 2) * (1 - 2 * (i % 2))


def kernel(
    sizes,
    vec, diag, blocks, rows_s, cols_s, count_s,
    out_x, out_l,
    s_in, s_nn, s_tt, d_in,
    x_send, d_send, t_send, g_send,
    rg, cg, cs, rs, gr,
    row_in, col_in, solve,
    in_sem,
    rg_ss, cg_ss, cs_ss, rs_ss, gr_ss,
    rg_rs, cg_rs, cs_rs, rs_rs, gr_rs,
    fr, f_send, f_ss, f_rs,
):
    n_x, n_l, n_k, n_hi, n_lo = sizes
    n_row, n_col = n_x * n_l * n_k, n_hi * n_lo
    slots = rows_s.shape[0]
    k, width = x_send.shape
    r = lax.axis_index("row")
    c = lax.axis_index("col")
    hi = c // n_lo
    lo = lax.rem(c, n_lo)
    x = r // (n_l * n_k)
    yl = lax.rem(r // n_k, n_l)
    core = lax.rem(r, n_k)

    def each_row(body):
        inner = n_l * n_k
        tails = [
            lax.rem(yl + far_first(n_l, i // n_k), n_l) * n_k + lax.rem(core + far_first(n_k, i % n_k), n_k)
            for i in range(inner)
        ]

        def outer(a, _):
            base = lax.rem(x + far_first(n_x, a), n_x) * inner
            for i in range(inner):
                body(base + tails[i])
            return 0

        lax.fori_loop(0, n_x - 1, outer, 0)
        for i in range(inner - 1):
            body(x * inner + tails[i])

    def each_col(body):
        tails = [lax.rem(lo + far_first(n_lo, i), n_lo) for i in range(n_lo)]

        def outer(a, _):
            base = lax.rem(hi + far_first(n_hi, a), n_hi) * n_lo
            for i in range(n_lo):
                body(base + tails[i])
            return 0

        lax.fori_loop(0, n_hi - 1, outer, 0)
        for i in range(n_lo - 1):
            body(hi * n_lo + tails[i])

    barrier = pltpu.get_barrier_semaphore()
    each_col(lambda q: pl.semaphore_signal(barrier, inc=1, device_id=(r, q), device_id_type=MESH))
    each_row(lambda q: pl.semaphore_signal(barrier, inc=1, device_id=(q, c), device_id_type=MESH))

    load = [
        pltpu.make_async_copy(blocks, s_in, in_sem.at[0]),
        pltpu.make_async_copy(vec, x_send, in_sem.at[1]),
        pltpu.make_async_copy(diag, d_in, in_sem.at[2]),
    ]
    for copy in load:
        copy.start()
    for copy in load:
        copy.wait()
    live = count_s[0, 0]
    for b in range(slots):
        keep = jnp.where(b < live, 1.0, 0.0).astype(F32)
        s = s_in[b] * keep
        t = jnp.transpose(s)
        s_hi = s.astype(BF16)
        s_nn[b, :, :width] = s_hi
        s_nn[b, :, width:] = (s - s_hi.astype(F32)).astype(BF16)
        t_hi = t.astype(BF16)
        s_tt[b, :, :width] = t_hi
        s_tt[b, :, width:] = (t - t_hi.astype(F32)).astype(BF16)

    row = lax.broadcasted_iota(jnp.int32, (k, width), 0)
    lane = lax.broadcasted_iota(jnp.int32, (k, width), 1)
    for j in range(k):
        solve[j] = jnp.where(row == j, 1.0, 0.0)
    g_send[...] = jnp.zeros_like(g_send)
    f_send[...] = jnp.zeros_like(f_send)
    pl.semaphore_wait(barrier, n_row + n_col - 2)

    def to_row(q, src, dst, send_sem, recv_sem):
        pltpu.make_async_remote_copy(
            src_ref=src, dst_ref=dst, send_sem=send_sem, recv_sem=recv_sem,
            device_id=(q, c), device_id_type=MESH,
        ).start()

    def to_col(q, src, dst, send_sem, recv_sem):
        pltpu.make_async_remote_copy(
            src_ref=src, dst_ref=dst, send_sem=send_sem, recv_sem=recv_sem,
            device_id=(r, q), device_id_type=MESH,
        ).start()

    def drain(pieces, sem):
        pltpu.make_async_copy(pieces, pieces, sem).wait()

    def gather_row(p):
        each_row(lambda q: to_row(q, x_send, rg.at[p, r], rg_ss, rg_rs.at[p]))

    def gather_col(p):
        each_col(lambda q: to_col(q, x_send, cg.at[p, c], cg_ss, cg_rs.at[p]))

    def solved(pieces):
        terms = [solve[j][None] * pieces[:, j : j + 1, :] for j in range(k)]
        return tree_sum(terms)

    def take_in(source, p, n, kept):
        for q in range(0, n, 8):
            m = min(8, n - q)
            w = solved(source[p, q : q + m])
            w_hi = w.astype(BF16).astype(F32)
            kept[q : q + m] = jnp.concatenate([w_hi, w - w_hi], axis=1).astype(BF16)

    def gram_kept():
        both = jnp.concatenate([col_in[q] for q in range(n_col)], axis=1)
        dims = (((1,), (1,)), ((), ()))
        a = lax.dot_general(both, both[:k], dims, preferred_element_type=F32)
        b = lax.dot_general(both, both[k:], dims, preferred_element_type=F32)
        return (a[:k] + (a[k:] + b[:k])) + b[k:]

    def pick(parts, place, q):
        return tree_sum(jnp.where(place[b] == q, parts[b], 0.0) for b in range(slots))

    def wait_pieces(buf, p, n, sem):
        drain(buf.at[p, pl.ds(0, n - 1)], sem)

    gather_row(0)
    gather_col(0)
    rg[0, r] = x_send[...]
    cg[0, c] = x_send[...]

    def step(t, _):
        p = lax.rem(t, 2)
        later = 1 - p
        at_row = [rows_s[b] for b in range(slots)]
        at_col = [cols_s[b] for b in range(slots)]

        wait_pieces(rg, p, n_row, rg_rs.at[p])
        take_in(rg, p, n_row, row_in)
        direct = [product(row_in[at_col[b]], s_tt[b]) for b in range(slots)]

        def scatter_col(q):
            d_send[q] = pick(direct, at_row, q)
            to_col(q, d_send.at[q], cs.at[p, c], cs_ss, cs_rs.at[p])

        each_col(scatter_col)
        cs[p, c] = pick(direct, at_row, c)
        own = d_in[...] * tree_sum(solve[j] * x_send[j : j + 1, :] for j in range(k))

        wait_pieces(cg, p, n_col, cg_rs.at[p])
        take_in(cg, p, n_col, col_in)
        trans = [product(col_in[at_row[b]], s_nn[b]) for b in range(slots)]

        def scatter_row(q):
            t_send[q] = pick(trans, at_col, q)
            to_row(q, t_send.at[q], rs.at[p, r], rs_ss, rs_rs.at[p])

        each_row(scatter_row)
        rs[p, r] = pick(trans, at_col, r)
        g_send[:, :k] = gram_kept()
        each_row(lambda q: to_row(q, g_send, gr.at[p, r], gr_ss, gr_rs.at[p]))
        gr[p, r] = g_send[...]

        wait_pieces(rg, p, n_row, rg_ss)
        wait_pieces(cg, p, n_col, cg_ss)
        wait_pieces(cs, p, n_col, cs_rs.at[p])
        own = own + tree_sum(cs[p, i] for i in range(n_col))
        wait_pieces(rs, p, n_row, rs_rs.at[p])
        images = own + tree_sum(rs[p, i] for i in range(n_row))
        x_send[...] = images

        @pl.when(t < ITERS - 1)
        def _():
            gather_row(later)

        gather_col(later)
        rg[later, r] = images
        cg[later, c] = images

        wait_pieces(gr, p, n_row, gr_rs.at[p])
        gram = tree_sum(gr[p, i] for i in range(n_row))
        gram = jnp.where(t == 0, jnp.where(row == lane, 1.0, 0.0), gram)
        columns = columns_of(factor(gram)[1])
        for j in range(k):
            solve[j] = columns[j]
        wait_pieces(cs, p, n_col, cs_ss)
        wait_pieces(rs, p, n_row, rs_ss)
        wait_pieces(gr, p, n_row, gr_ss)
        return 0

    lax.fori_loop(0, ITERS, step, 0)

    last = ITERS % 2
    wait_pieces(cg, last, n_col, cg_rs.at[last])
    take_in(cg, last, n_col, col_in)
    f_send[:, :k] = gram_kept()
    each_row(lambda q: to_row(q, f_send, fr.at[r], f_ss, f_rs))
    fr[r] = f_send[...]
    images = tree_sum(solve[j] * x_send[j : j + 1, :] for j in range(k))
    drain(fr.at[pl.ds(0, n_row - 1)], f_rs)
    lower, inverse = factor(tree_sum(fr[i] for i in range(n_row)))
    out_x[...] = apply(columns_of(inverse), images)
    out_l[...] = lower[:, :k]
    wait_pieces(cg, last, n_col, cg_ss)
    drain(fr.at[pl.ds(0, n_row - 1)], f_ss)


def solution(mesh):
    n_row, n_col = mesh.shape["row"], mesh.shape["col"]
    n_k = 2 if n_row % 2 == 0 else 1
    n_l = 2 if n_row % 4 == 0 else 1
    n_x = n_row // (n_k * n_l)
    n_hi = 4 if n_col % 8 == 0 else 2
    n_lo = n_col // n_hi

    def shards(vectors, diagonal, blocks, block_rows, block_cols, counts):
        k, width = vectors.shape
        slots = blocks.shape[2]
        piece = (k, width)
        vmem = pl.BlockSpec(memory_space=pltpu.VMEM)
        smem = pl.BlockSpec(memory_space=pltpu.SMEM)
        left = pl.BlockSpec(memory_space=pl.ANY)
        dma = pltpu.SemaphoreType.DMA
        return pl.pallas_call(
            functools.partial(kernel, (n_x, n_l, n_k, n_hi, n_lo)),
            out_shape=(jax.ShapeDtypeStruct(piece, F32), jax.ShapeDtypeStruct((k, k), F32)),
            in_specs=[left, left, left, smem, smem, smem],
            out_specs=(vmem, vmem),
            scratch_shapes=[
                pltpu.VMEM((slots, width, width), F32),
                pltpu.VMEM((slots, width, 2 * width), BF16),
                pltpu.VMEM((slots, width, 2 * width), BF16),
                pltpu.VMEM((1, width), F32),
                pltpu.VMEM(piece, F32),
                pltpu.VMEM((n_col,) + piece, F32),
                pltpu.VMEM((n_row,) + piece, F32),
                pltpu.VMEM(piece, F32),
                pltpu.VMEM((2, n_row) + piece, F32),
                pltpu.VMEM((2, n_col) + piece, F32),
                pltpu.VMEM((2, n_col) + piece, F32),
                pltpu.VMEM((2, n_row) + piece, F32),
                pltpu.VMEM((2, n_row) + piece, F32),
                pltpu.VMEM((n_row, 2 * k, width), BF16),
                pltpu.VMEM((n_col, 2 * k, width), BF16),
                pltpu.VMEM((k,) + piece, F32),
                dma((3,)),
                dma, dma, dma, dma, dma,
                dma((2,)), dma((2,)), dma((2,)), dma((2,)), dma((2,)),
                pltpu.VMEM((n_row,) + piece, F32),
                pltpu.VMEM(piece, F32),
                dma,
                dma,
            ],
            compiler_params=pltpu.CompilerParams(
                collective_id=0, has_side_effects=True, vmem_limit_bytes=60 * 1024 * 1024
            ),
        )(
            vectors, diagonal.reshape(1, width), blocks.reshape(slots, width, width),
            block_rows.reshape(slots), block_cols.reshape(slots), counts,
        )

    return jax.shard_map(
        shards,
        mesh=mesh,
        in_specs=(
            P(None, ("row", "col")),
            P(("row", "col")),
            P("row", "col", None, None, None),
            P("row", "col", None),
            P("row", "col", None),
            P("row", "col"),
        ),
        out_specs=(P(None, ("row", "col")), P()),
        check_vma=False,
    )
```

```python
import functools

import jax
import jax.numpy as jnp
from jax import lax
from jax.experimental import pallas as pl
from jax.experimental.pallas import tpu as pltpu
from jax.sharding import PartitionSpec as P

ITERS = 4
MESH = pl.DeviceIdType.MESH
F32 = jnp.float32
BF16 = jnp.bfloat16


def split_rows(x):
    hi = x.astype(BF16).astype(F32)
    return jnp.concatenate([hi, x - hi], axis=0).astype(BF16)


def product(both, pair):
    out = jnp.dot(both, pair, preferred_element_type=F32)
    k = both.shape[0] // 2
    n = pair.shape[1] // 2
    return (out[:k, :n] + (out[k:, :n] + out[:k, n:])) + out[k:, n:]


def gram_of(wide):
    both = split_rows(wide)
    k = wide.shape[0]
    dims = (((1,), (1,)), ((), ()))
    high = both[:k]
    low = both[k:]
    a = lax.dot_general(both, high, dims, preferred_element_type=F32)
    b = lax.dot_general(both, low, dims, preferred_element_type=F32)
    return (a[:k] + (a[k:] + b[:k])) + b[k:]


def factor(gram):
    k, lanes = gram.shape
    row = lax.broadcasted_iota(jnp.int32, (k, lanes), 0)
    lane = lax.broadcasted_iota(jnp.int32, (k, lanes), 1)
    a = jnp.where(lane < k, gram, jnp.where(lane - k == row, 1.0, 0.0))
    lower = jnp.zeros((k, lanes), F32)
    scale = jnp.zeros((k, lanes), F32)
    for j in range(k):
        col = jnp.broadcast_to(a[:, j : j + 1], (k, lanes))
        pivot_row = jnp.broadcast_to(a[j : j + 1, :], (k, lanes))
        pivot = jnp.broadcast_to(col[j : j + 1, :], (k, lanes))
        root = lax.rsqrt(pivot)
        a = a - jnp.where(row > j, col * (1.0 / pivot), 0.0) * pivot_row
        lower = jnp.where((lane == j) & (row >= j), col * root, lower)
        scale = jnp.where(row == j, root, scale)
    return lower, a * scale


def columns_of(inverse):
    k, lanes = inverse.shape
    return [jnp.broadcast_to(inverse[:, k + j : k + j + 1], (k, lanes)) for j in range(k)]


def apply(columns, values):
    k, lanes = values.shape
    terms = [columns[j] * jnp.broadcast_to(values[j : j + 1, :], (k, lanes)) for j in range(k)]
    while len(terms) > 1:
        terms = [a + b for a, b in zip(terms[::2], terms[1::2])]
    return terms[0]


def tree_sum(values):
    values = list(values)
    while len(values) > 1:
        pairs = [a + b for a, b in zip(values[::2], values[1::2])]
        if len(values) % 2:
            pairs.append(values[-1])
        values = pairs
    return values[0]


def far_first(n, i):
    return n // 2 + ((i + 1) // 2) * (1 - 2 * (i % 2))


def kernel(
    sizes,
    vec, diag, blocks, rows_in, cols_in, count_in,
    out_x, out_l,
    s_in, s_nn, s_tt, d_in, rows_s, cols_s, count_s,
    x_send, d_send, t_send, g_send,
    rg, cg, cs, rs, gr,
    row_in, col_in, col_raw, solve,
    in_sem,
    rg_ss, cg_ss, cs_ss, rs_ss, gr_ss,
    rg_rs, cg_rs, cs_rs, rs_rs, gr_rs,
    fr, f_send, f_ss, f_rs,
):
    n_x, n_l, n_k, n_hi, n_lo = sizes
    n_row, n_col = n_x * n_l * n_k, n_hi * n_lo
    slots = blocks.shape[0]
    k, width = x_send.shape
    r = lax.axis_index("row")
    c = lax.axis_index("col")
    hi = c // n_lo
    lo = lax.rem(c, n_lo)
    x = r // (n_l * n_k)
    yl = lax.rem(r // n_k, n_l)
    core = lax.rem(r, n_k)

    def each_row(body):
        inner = n_l * n_k
        tails = [
            lax.rem(yl + far_first(n_l, i // n_k), n_l) * n_k + lax.rem(core + far_first(n_k, i % n_k), n_k)
            for i in range(inner)
        ]

        def outer(a, _):
            base = lax.rem(x + far_first(n_x, a), n_x) * inner
            for i in range(inner):
                body(base + tails[i])
            return 0

        lax.fori_loop(0, n_x - 1, outer, 0)
        for i in range(inner - 1):
            body(x * inner + tails[i])

    def each_col(body):
        tails = [lax.rem(lo + far_first(n_lo, i), n_lo) for i in range(n_lo)]

        def outer(a, _):
            base = lax.rem(hi + far_first(n_hi, a), n_hi) * n_lo
            for i in range(n_lo):
                body(base + tails[i])
            return 0

        lax.fori_loop(0, n_hi - 1, outer, 0)
        for i in range(n_lo - 1):
            body(hi * n_lo + tails[i])

    barrier = pltpu.get_barrier_semaphore()
    each_col(lambda q: pl.semaphore_signal(barrier, inc=1, device_id=(r, q), device_id_type=MESH))
    each_row(lambda q: pl.semaphore_signal(barrier, inc=1, device_id=(q, c), device_id_type=MESH))

    load = [
        pltpu.make_async_copy(blocks, s_in, in_sem.at[0]),
        pltpu.make_async_copy(vec, x_send, in_sem.at[1]),
        pltpu.make_async_copy(diag, d_in, in_sem.at[2]),
        pltpu.make_async_copy(rows_in, rows_s, in_sem.at[3]),
        pltpu.make_async_copy(cols_in, cols_s, in_sem.at[4]),
        pltpu.make_async_copy(count_in, count_s, in_sem.at[5]),
    ]
    for copy in load:
        copy.start()
    for copy in load:
        copy.wait()
    live = count_s[0, 0]
    for b in range(slots):
        keep = jnp.where(b < live, 1.0, 0.0).astype(F32)
        s = s_in[b] * keep
        t = jnp.transpose(s)
        s_hi = s.astype(BF16)
        s_nn[b, :, :width] = s_hi
        s_nn[b, :, width:] = (s - s_hi.astype(F32)).astype(BF16)
        t_hi = t.astype(BF16)
        s_tt[b, :, :width] = t_hi
        s_tt[b, :, width:] = (t - t_hi.astype(F32)).astype(BF16)

    row = lax.broadcasted_iota(jnp.int32, (k, width), 0)
    lane = lax.broadcasted_iota(jnp.int32, (k, width), 1)
    for j in range(k):
        solve[j] = jnp.where(row == j, 1.0, 0.0)
    g_send[...] = jnp.zeros_like(g_send)
    f_send[...] = jnp.zeros_like(f_send)
    pl.semaphore_wait(barrier, n_row + n_col - 2)

    def to_row(q, src, dst, send_sem, recv_sem):
        pltpu.make_async_remote_copy(
            src_ref=src, dst_ref=dst, send_sem=send_sem, recv_sem=recv_sem,
            device_id=(q, c), device_id_type=MESH,
        ).start()

    def to_col(q, src, dst, send_sem, recv_sem):
        pltpu.make_async_remote_copy(
            src_ref=src, dst_ref=dst, send_sem=send_sem, recv_sem=recv_sem,
            device_id=(r, q), device_id_type=MESH,
        ).start()

    def drain(pieces, sem):
        pltpu.make_async_copy(pieces, pieces, sem).wait()

    def gather_row(p):
        each_row(lambda q: to_row(q, x_send, rg.at[p, r], rg_ss, rg_rs.at[p]))

    def gather_col(p):
        each_col(lambda q: to_col(q, x_send, cg.at[p, c], cg_ss, cg_rs.at[p]))

    def solved(pieces):
        terms = [solve[j][None] * pieces[:, j : j + 1, :] for j in range(k)]
        return tree_sum(terms)

    def take_in(source, p, n, kept):
        for q in range(0, n, 8):
            m = min(8, n - q)
            w = solved(source[p, q : q + m])
            w_hi = w.astype(BF16).astype(F32)
            kept[q : q + m] = jnp.concatenate([w_hi, w - w_hi], axis=1).astype(BF16)

    def gram_kept():
        both = jnp.concatenate([col_in[q] for q in range(n_col)], axis=1)
        dims = (((1,), (1,)), ((), ()))
        a = lax.dot_general(both, both[:k], dims, preferred_element_type=F32)
        b = lax.dot_general(both, both[k:], dims, preferred_element_type=F32)
        return (a[:k] + (a[k:] + b[:k])) + b[k:]

    def pick(parts, place, q):
        return tree_sum(jnp.where(place[b] == q, parts[b], 0.0) for b in range(slots))

    def wait_pieces(buf, p, n, sem):
        drain(buf.at[p, pl.ds(0, n - 1)], sem)

    gather_row(0)
    gather_col(0)
    rg[0, r] = x_send[...]
    cg[0, c] = x_send[...]

    def step(t, _):
        p = lax.rem(t, 2)
        later = 1 - p
        at_row = [rows_s[0, b] for b in range(slots)]
        at_col = [cols_s[0, b] for b in range(slots)]

        wait_pieces(rg, p, n_row, rg_rs.at[p])
        take_in(rg, p, n_row, row_in)
        direct = [product(row_in[at_col[b]], s_tt[b]) for b in range(slots)]

        def scatter_col(q):
            d_send[q] = pick(direct, at_row, q)
            to_col(q, d_send.at[q], cs.at[p, c], cs_ss, cs_rs.at[p])

        each_col(scatter_col)
        cs[p, c] = pick(direct, at_row, c)
        own = d_in[...] * tree_sum(solve[j] * x_send[j : j + 1, :] for j in range(k))

        wait_pieces(cg, p, n_col, cg_rs.at[p])
        for q in range(n_col):
            col_raw[q] = cg[p, q]
        used = [split_rows(solved(col_raw[at_row[b]][None])[0]) for b in range(slots)]
        trans = [product(used[b], s_nn[b]) for b in range(slots)]

        def scatter_row(q):
            t_send[q] = pick(trans, at_col, q)
            to_row(q, t_send.at[q], rs.at[p, r], rs_ss, rs_rs.at[p])

        each_row(scatter_row)
        rs[p, r] = pick(trans, at_col, r)
        take_in(cg, p, n_col, col_in)
        g_send[:, :k] = gram_kept()
        each_row(lambda q: to_row(q, g_send, gr.at[p, r], gr_ss, gr_rs.at[p]))
        gr[p, r] = g_send[...]

        wait_pieces(rg, p, n_row, rg_ss)
        wait_pieces(cg, p, n_col, cg_ss)
        wait_pieces(cs, p, n_col, cs_rs.at[p])
        own = own + tree_sum(cs[p, i] for i in range(n_col))
        wait_pieces(rs, p, n_row, rs_rs.at[p])
        images = own + tree_sum(rs[p, i] for i in range(n_row))
        x_send[...] = images

        @pl.when(t < ITERS - 1)
        def _():
            gather_row(later)

        gather_col(later)
        rg[later, r] = images
        cg[later, c] = images

        wait_pieces(gr, p, n_row, gr_rs.at[p])
        gram = tree_sum(gr[p, i] for i in range(n_row))
        gram = jnp.where(t == 0, jnp.where(row == lane, 1.0, 0.0), gram)
        columns = columns_of(factor(gram)[1])
        for j in range(k):
            solve[j] = columns[j]
        wait_pieces(cs, p, n_col, cs_ss)
        wait_pieces(rs, p, n_row, rs_ss)
        wait_pieces(gr, p, n_row, gr_ss)
        return 0

    lax.fori_loop(0, ITERS, step, 0)

    last = ITERS % 2
    wait_pieces(cg, last, n_col, cg_rs.at[last])
    take_in(cg, last, n_col, col_in)
    f_send[:, :k] = gram_kept()
    each_row(lambda q: to_row(q, f_send, fr.at[r], f_ss, f_rs))
    fr[r] = f_send[...]
    images = tree_sum(solve[j] * x_send[j : j + 1, :] for j in range(k))
    drain(fr.at[pl.ds(0, n_row - 1)], f_rs)
    lower, inverse = factor(tree_sum(fr[i] for i in range(n_row)))
    out_x[...] = apply(columns_of(inverse), images)
    out_l[...] = lower[:, :k]
    wait_pieces(cg, last, n_col, cg_ss)
    drain(fr.at[pl.ds(0, n_row - 1)], f_ss)


def solution(mesh):
    n_row, n_col = mesh.shape["row"], mesh.shape["col"]
    n_k = 2 if n_row % 2 == 0 else 1
    n_l = 2 if n_row % 4 == 0 else 1
    n_x = n_row // (n_k * n_l)
    n_hi = 4 if n_col % 8 == 0 else 2
    n_lo = n_col // n_hi

    def shards(vectors, diagonal, blocks, block_rows, block_cols, counts):
        k, width = vectors.shape
        slots = blocks.shape[2]
        piece = (k, width)
        vmem = pl.BlockSpec(memory_space=pltpu.VMEM)
        left = pl.BlockSpec(memory_space=pl.ANY)
        dma = pltpu.SemaphoreType.DMA
        return pl.pallas_call(
            functools.partial(kernel, (n_x, n_l, n_k, n_hi, n_lo)),
            out_shape=(pltpu.VMEM(piece, F32), pltpu.VMEM((k, k), F32)),
            in_specs=[left] * 6,
            out_specs=(vmem, vmem),
            scratch_shapes=[
                pltpu.VMEM((slots, width, width), F32),
                pltpu.VMEM((slots, width, 2 * width), BF16),
                pltpu.VMEM((slots, width, 2 * width), BF16),
                pltpu.VMEM((1, width), F32),
                pltpu.SMEM((1, slots), jnp.int32),
                pltpu.SMEM((1, slots), jnp.int32),
                pltpu.SMEM((1, 1), jnp.int32),
                pltpu.VMEM(piece, F32),
                pltpu.VMEM((n_col,) + piece, F32),
                pltpu.VMEM((n_row,) + piece, F32),
                pltpu.VMEM(piece, F32),
                pltpu.VMEM((2, n_row) + piece, F32),
                pltpu.VMEM((2, n_col) + piece, F32),
                pltpu.VMEM((2, n_col) + piece, F32),
                pltpu.VMEM((2, n_row) + piece, F32),
                pltpu.VMEM((2, n_row) + piece, F32),
                pltpu.VMEM((n_row, 2 * k, width), BF16),
                pltpu.VMEM((n_col, 2 * k, width), BF16),
                pltpu.VMEM((n_col,) + piece, F32),
                pltpu.VMEM((k,) + piece, F32),
                dma((6,)),
                dma, dma, dma, dma, dma,
                dma((2,)), dma((2,)), dma((2,)), dma((2,)), dma((2,)),
                pltpu.VMEM((n_row,) + piece, F32),
                pltpu.VMEM(piece, F32),
                dma,
                dma,
            ],
            compiler_params=pltpu.CompilerParams(
                collective_id=0, has_side_effects=True, vmem_limit_bytes=60 * 1024 * 1024
            ),
        )(
            vectors, diagonal.reshape(1, width), blocks.reshape(slots, width, width),
            block_rows.reshape(1, slots), block_cols.reshape(1, slots), counts,
        )

    return jax.shard_map(
        shards,
        mesh=mesh,
        in_specs=(
            P(None, ("row", "col")),
            P(("row", "col")),
            P("row", "col", None, None, None),
            P("row", "col", None),
            P("row", "col", None),
            P("row", "col"),
        ),
        out_specs=(P(None, ("row", "col")), P()),
        check_vma=False,
    )
```

```python
import functools

import jax
import jax.numpy as jnp
from jax import lax
from jax.experimental import pallas as pl
from jax.experimental.pallas import tpu as pltpu
from jax.sharding import PartitionSpec as P

ITERS = 4
MESH = pl.DeviceIdType.MESH
F32 = jnp.float32
BF16 = jnp.bfloat16


def split_rows(x):
    hi = x.astype(BF16).astype(F32)
    return jnp.concatenate([hi, x - hi], axis=0).astype(BF16)


def product(both, pair):
    out = jnp.dot(both, pair, preferred_element_type=F32)
    k = both.shape[0] // 2
    n = pair.shape[1] // 2
    return (out[:k, :n] + (out[k:, :n] + out[:k, n:])) + out[k:, n:]


def gram_of(wide):
    both = split_rows(wide)
    k = wide.shape[0]
    dims = (((1,), (1,)), ((), ()))
    high = both[:k]
    low = both[k:]
    a = lax.dot_general(both, high, dims, preferred_element_type=F32)
    b = lax.dot_general(both, low, dims, preferred_element_type=F32)
    return (a[:k] + (a[k:] + b[:k])) + b[k:]


def factor(gram):
    k, lanes = gram.shape
    row = lax.broadcasted_iota(jnp.int32, (k, lanes), 0)
    lane = lax.broadcasted_iota(jnp.int32, (k, lanes), 1)
    a = jnp.where(lane < k, gram, jnp.where(lane - k == row, 1.0, 0.0))
    lower = jnp.zeros((k, lanes), F32)
    scale = jnp.zeros((k, lanes), F32)
    for j in range(k):
        col = jnp.broadcast_to(a[:, j : j + 1], (k, lanes))
        pivot_row = jnp.broadcast_to(a[j : j + 1, :], (k, lanes))
        pivot = jnp.broadcast_to(col[j : j + 1, :], (k, lanes))
        root = lax.rsqrt(pivot)
        a = a - jnp.where(row > j, col * (1.0 / pivot), 0.0) * pivot_row
        lower = jnp.where((lane == j) & (row >= j), col * root, lower)
        scale = jnp.where(row == j, root, scale)
    return lower, a * scale


def columns_of(inverse):
    k, lanes = inverse.shape
    return [jnp.broadcast_to(inverse[:, k + j : k + j + 1], (k, lanes)) for j in range(k)]


def apply(columns, values):
    k, lanes = values.shape
    terms = [columns[j] * jnp.broadcast_to(values[j : j + 1, :], (k, lanes)) for j in range(k)]
    while len(terms) > 1:
        terms = [a + b for a, b in zip(terms[::2], terms[1::2])]
    return terms[0]


def tree_sum(values):
    values = list(values)
    while len(values) > 1:
        pairs = [a + b for a, b in zip(values[::2], values[1::2])]
        if len(values) % 2:
            pairs.append(values[-1])
        values = pairs
    return values[0]


def far_first(n, i):
    return n // 2 + ((i + 1) // 2) * (1 - 2 * (i % 2))


def kernel(
    sizes,
    vec, diag, blocks, rows_in, cols_in, count_in,
    out_x, out_l,
    s_in, s_nn, s_tt, d_in, rows_s, cols_s, count_s,
    x_send, d_send, t_send, g_send,
    rg, cg, cs, rs, gr,
    row_in, col_in, col_raw, solve,
    in_sem,
    rg_ss, cg_ss, yg_ss, zg_ss, cs_ss, rs_ss, gr_ss,
    rg_rs, cg_rs, yg_rs, zg_rs, cs_rs, rs_rs, gr_rs,
    fr, f_send, f_ss, f_rs,
):
    n_x, n_l, n_k, n_hi, n_lo = sizes
    n_row, n_col = n_x * n_l * n_k, n_hi * n_lo
    slots = blocks.shape[0]
    k, width = x_send.shape
    r = lax.axis_index("row")
    c = lax.axis_index("col")
    hi = c // n_lo
    lo = lax.rem(c, n_lo)
    x = r // (n_l * n_k)
    yl = lax.rem(r // n_k, n_l)
    core = lax.rem(r, n_k)

    def each_row(body):
        inner = n_l * n_k
        tails = [
            lax.rem(yl + far_first(n_l, i // n_k), n_l) * n_k + lax.rem(core + far_first(n_k, i % n_k), n_k)
            for i in range(inner)
        ]

        def outer(a, _):
            base = lax.rem(x + far_first(n_x, a), n_x) * inner
            for i in range(inner):
                body(base + tails[i])
            return 0

        lax.fori_loop(0, n_x - 1, outer, 0)
        for i in range(inner - 1):
            body(x * inner + tails[i])

    def each_col(body):
        tails = [lax.rem(lo + far_first(n_lo, i), n_lo) for i in range(n_lo)]

        def outer(a, _):
            base = lax.rem(hi + far_first(n_hi, a), n_hi) * n_lo
            for i in range(n_lo):
                body(base + tails[i])
            return 0

        lax.fori_loop(0, n_hi - 1, outer, 0)
        for i in range(n_lo - 1):
            body(hi * n_lo + tails[i])

    barrier = pltpu.get_barrier_semaphore()
    each_col(lambda q: pl.semaphore_signal(barrier, inc=1, device_id=(r, q), device_id_type=MESH))
    each_row(lambda q: pl.semaphore_signal(barrier, inc=1, device_id=(q, c), device_id_type=MESH))

    load = [
        pltpu.make_async_copy(blocks, s_in, in_sem.at[0]),
        pltpu.make_async_copy(vec, x_send, in_sem.at[1]),
        pltpu.make_async_copy(diag, d_in, in_sem.at[2]),
        pltpu.make_async_copy(rows_in, rows_s, in_sem.at[3]),
        pltpu.make_async_copy(cols_in, cols_s, in_sem.at[4]),
        pltpu.make_async_copy(count_in, count_s, in_sem.at[5]),
    ]
    for copy in load:
        copy.start()
    for copy in load:
        copy.wait()
    live = count_s[0, 0]
    for b in range(slots):
        keep = jnp.where(b < live, 1.0, 0.0).astype(F32)
        s = s_in[b] * keep
        t = jnp.transpose(s)
        s_hi = s.astype(BF16)
        s_nn[b, :, :width] = s_hi
        s_nn[b, :, width:] = (s - s_hi.astype(F32)).astype(BF16)
        t_hi = t.astype(BF16)
        s_tt[b, :, :width] = t_hi
        s_tt[b, :, width:] = (t - t_hi.astype(F32)).astype(BF16)

    row = lax.broadcasted_iota(jnp.int32, (k, width), 0)
    lane = lax.broadcasted_iota(jnp.int32, (k, width), 1)
    for j in range(k):
        solve[j] = jnp.where(row == j, 1.0, 0.0)
    g_send[...] = jnp.zeros_like(g_send)
    f_send[...] = jnp.zeros_like(f_send)
    pl.semaphore_wait(barrier, n_row + n_col - 2)

    def to_row(q, src, dst, send_sem, recv_sem):
        pltpu.make_async_remote_copy(
            src_ref=src, dst_ref=dst, send_sem=send_sem, recv_sem=recv_sem,
            device_id=(q, c), device_id_type=MESH,
        ).start()

    def to_col(q, src, dst, send_sem, recv_sem):
        pltpu.make_async_remote_copy(
            src_ref=src, dst_ref=dst, send_sem=send_sem, recv_sem=recv_sem,
            device_id=(r, q), device_id_type=MESH,
        ).start()

    def drain(pieces, sem):
        pltpu.make_async_copy(pieces, pieces, sem).wait()

    def gather_row(p):
        each_row(lambda q: to_row(q, x_send, rg.at[p, r], rg_ss, rg_rs.at[p]))

    near = [d for d in range(1, n_lo) if min(d, n_lo - d) <= n_lo // 4]
    distant = [far_first(n_lo, i) for i in range(n_lo - 1) if far_first(n_lo, i) not in near]

    def own_column(p):
        for i in range(n_hi - 1):
            q = lax.rem(hi + far_first(n_hi, i), n_hi) * n_lo + lo
            to_col(q, x_send, cg.at[p, lo, hi], yg_ss, yg_rs.at[p])

    def far_columns(p):
        for i in range(n_hi):
            base = lax.rem(hi + far_first(n_hi, i), n_hi) * n_lo
            for d in distant:
                to_col(base + lax.rem(lo + d, n_lo), x_send, cg.at[p, lo, hi], cg_ss, cg_rs.at[p])

    def near_columns(p):
        drain(cg.at[p, 0, pl.ds(0, n_hi - 1)], yg_rs.at[p])
        for d in near:
            to_col(hi * n_lo + lax.rem(lo + d, n_lo), cg.at[p, lo], cg.at[p, lo], zg_ss, zg_rs.at[p])

    def drain_col(p, far_sem, near_sem):
        drain(cg.at[p, pl.ds(0, len(distant))], far_sem)
        drain(cg.at[p, pl.ds(0, len(near))], near_sem)

    def solved(pieces):
        terms = [solve[j][None] * pieces[:, j : j + 1, :] for j in range(k)]
        return tree_sum(terms)

    def take_in(source, n, kept):
        for q in range(0, n, 8):
            m = min(8, n - q)
            w = solved(source[q : q + m])
            w_hi = w.astype(BF16).astype(F32)
            kept[q : q + m] = jnp.concatenate([w_hi, w - w_hi], axis=1).astype(BF16)

    def gram_kept():
        both = jnp.concatenate([col_in[q] for q in range(n_col)], axis=1)
        dims = (((1,), (1,)), ((), ()))
        a = lax.dot_general(both, both[:k], dims, preferred_element_type=F32)
        b = lax.dot_general(both, both[k:], dims, preferred_element_type=F32)
        return (a[:k] + (a[k:] + b[:k])) + b[k:]

    def pick(parts, place, q):
        return tree_sum(jnp.where(place[b] == q, parts[b], 0.0) for b in range(slots))

    def wait_pieces(buf, p, n, sem):
        drain(buf.at[p, pl.ds(0, n - 1)], sem)

    rg[0, r] = x_send[...]
    cg[0, lo, hi] = x_send[...]
    own_column(0)
    gather_row(0)
    far_columns(0)

    def step(t, _):
        p = lax.rem(t, 2)
        later = 1 - p
        at_row = [rows_s[0, b] for b in range(slots)]
        kept_at = [lax.rem(q, n_lo) * n_hi + q // n_lo for q in at_row]
        at_col = [cols_s[0, b] for b in range(slots)]

        near_columns(p)

        wait_pieces(rg, p, n_row, rg_rs.at[p])
        take_in(rg.at[p], n_row, row_in)
        direct = [product(row_in[at_col[b]], s_tt[b]) for b in range(slots)]

        def scatter_col(q):
            d_send[q] = pick(direct, at_row, q)
            to_col(q, d_send.at[q], cs.at[p, c], cs_ss, cs_rs.at[p])

        each_col(scatter_col)
        cs[p, c] = pick(direct, at_row, c)
        own = d_in[...] * tree_sum(solve[j] * x_send[j : j + 1, :] for j in range(k))

        drain_col(p, cg_rs.at[p], zg_rs.at[p])
        for q in range(n_col):
            col_raw[q] = cg[p, q // n_hi, q % n_hi]
        used = [split_rows(solved(col_raw[kept_at[b]][None])[0]) for b in range(slots)]
        trans = [product(used[b], s_nn[b]) for b in range(slots)]

        def scatter_row(q):
            t_send[q] = pick(trans, at_col, q)
            to_row(q, t_send.at[q], rs.at[p, r], rs_ss, rs_rs.at[p])

        each_row(scatter_row)
        rs[p, r] = pick(trans, at_col, r)
        take_in(col_raw, n_col, col_in)
        g_send[:, :k] = gram_kept()
        each_row(lambda q: to_row(q, g_send, gr.at[p, r], gr_ss, gr_rs.at[p]))
        gr[p, r] = g_send[...]

        wait_pieces(rg, p, n_row, rg_ss)
        drain(cg.at[p, 0, pl.ds(0, n_hi - 1)], yg_ss)
        drain_col(p, cg_ss, zg_ss)
        wait_pieces(cs, p, n_col, cs_rs.at[p])
        own = own + tree_sum(cs[p, i] for i in range(n_col))
        wait_pieces(rs, p, n_row, rs_rs.at[p])
        images = own + tree_sum(rs[p, i] for i in range(n_row))
        x_send[...] = images

        rg[later, r] = images
        cg[later, lo, hi] = images
        own_column(later)

        @pl.when(t < ITERS - 1)
        def _():
            gather_row(later)

        far_columns(later)

        wait_pieces(gr, p, n_row, gr_rs.at[p])
        gram = tree_sum(gr[p, i] for i in range(n_row))
        gram = jnp.where(t == 0, jnp.where(row == lane, 1.0, 0.0), gram)
        columns = columns_of(factor(gram)[1])
        for j in range(k):
            solve[j] = columns[j]
        wait_pieces(cs, p, n_col, cs_ss)
        wait_pieces(rs, p, n_row, rs_ss)
        wait_pieces(gr, p, n_row, gr_ss)
        return 0

    lax.fori_loop(0, ITERS, step, 0)

    last = ITERS % 2
    near_columns(last)
    drain_col(last, cg_rs.at[last], zg_rs.at[last])
    for q in range(n_col):
        col_raw[q] = cg[last, q // n_hi, q % n_hi]
    take_in(col_raw, n_col, col_in)
    f_send[:, :k] = gram_kept()
    each_row(lambda q: to_row(q, f_send, fr.at[r], f_ss, f_rs))
    fr[r] = f_send[...]
    images = tree_sum(solve[j] * x_send[j : j + 1, :] for j in range(k))
    drain(fr.at[pl.ds(0, n_row - 1)], f_rs)
    lower, inverse = factor(tree_sum(fr[i] for i in range(n_row)))
    out_x[...] = apply(columns_of(inverse), images)
    out_l[...] = lower[:, :k]
    drain(cg.at[last, 0, pl.ds(0, n_hi - 1)], yg_ss)
    drain_col(last, cg_ss, zg_ss)
    drain(fr.at[pl.ds(0, n_row - 1)], f_ss)


def solution(mesh):
    n_row, n_col = mesh.shape["row"], mesh.shape["col"]
    n_k = 2 if n_row % 2 == 0 else 1
    n_l = 2 if n_row % 4 == 0 else 1
    n_x = n_row // (n_k * n_l)
    n_hi = 4 if n_col % 8 == 0 else 2
    n_lo = n_col // n_hi

    def shards(vectors, diagonal, blocks, block_rows, block_cols, counts):
        k, width = vectors.shape
        slots = blocks.shape[2]
        piece = (k, width)
        vmem = pl.BlockSpec(memory_space=pltpu.VMEM)
        left = pl.BlockSpec(memory_space=pl.ANY)
        dma = pltpu.SemaphoreType.DMA
        return pl.pallas_call(
            functools.partial(kernel, (n_x, n_l, n_k, n_hi, n_lo)),
            out_shape=(pltpu.VMEM(piece, F32), pltpu.VMEM((k, k), F32)),
            in_specs=[left] * 6,
            out_specs=(vmem, vmem),
            scratch_shapes=[
                pltpu.VMEM((slots, width, width), F32),
                pltpu.VMEM((slots, width, 2 * width), BF16),
                pltpu.VMEM((slots, width, 2 * width), BF16),
                pltpu.VMEM((1, width), F32),
                pltpu.SMEM((1, slots), jnp.int32),
                pltpu.SMEM((1, slots), jnp.int32),
                pltpu.SMEM((1, 1), jnp.int32),
                pltpu.VMEM(piece, F32),
                pltpu.VMEM((n_col,) + piece, F32),
                pltpu.VMEM((n_row,) + piece, F32),
                pltpu.VMEM(piece, F32),
                pltpu.VMEM((2, n_row) + piece, F32),
                pltpu.VMEM((2, n_lo, n_hi) + piece, F32),
                pltpu.VMEM((2, n_col) + piece, F32),
                pltpu.VMEM((2, n_row) + piece, F32),
                pltpu.VMEM((2, n_row) + piece, F32),
                pltpu.VMEM((n_row, 2 * k, width), BF16),
                pltpu.VMEM((n_col, 2 * k, width), BF16),
                pltpu.VMEM((n_col,) + piece, F32),
                pltpu.VMEM((k,) + piece, F32),
                dma((6,)),
                dma, dma, dma, dma, dma, dma, dma,
                dma((2,)), dma((2,)), dma((2,)), dma((2,)), dma((2,)), dma((2,)), dma((2,)),
                pltpu.VMEM((n_row,) + piece, F32),
                pltpu.VMEM(piece, F32),
                dma,
                dma,
            ],
            compiler_params=pltpu.CompilerParams(
                collective_id=0, has_side_effects=True, vmem_limit_bytes=60 * 1024 * 1024
            ),
        )(
            vectors, diagonal.reshape(1, width), blocks.reshape(slots, width, width),
            block_rows.reshape(1, slots), block_cols.reshape(1, slots), counts,
        )

    return jax.shard_map(
        shards,
        mesh=mesh,
        in_specs=(
            P(None, ("row", "col")),
            P(("row", "col")),
            P("row", "col", None, None, None),
            P("row", "col", None),
            P("row", "col", None),
            P("row", "col"),
        ),
        out_specs=(P(None, ("row", "col")), P()),
        check_vma=False,
    )
```

```python
import functools

import jax
import jax.numpy as jnp
from jax import lax
from jax.experimental import pallas as pl
from jax.experimental.pallas import tpu as pltpu
from jax.sharding import PartitionSpec as P

ITERS = 4
MESH = pl.DeviceIdType.MESH
F32 = jnp.float32
BF16 = jnp.bfloat16


def split_rows(x):
    hi = x.astype(BF16).astype(F32)
    return jnp.concatenate([hi, x - hi], axis=0).astype(BF16)


def product(both, pair):
    out = jnp.dot(both, pair, preferred_element_type=F32)
    k = both.shape[0] // 2
    n = pair.shape[1] // 2
    return (out[:k, :n] + (out[k:, :n] + out[:k, n:])) + out[k:, n:]


def gram_of(wide):
    both = split_rows(wide)
    k = wide.shape[0]
    dims = (((1,), (1,)), ((), ()))
    high = both[:k]
    low = both[k:]
    a = lax.dot_general(both, high, dims, preferred_element_type=F32)
    b = lax.dot_general(both, low, dims, preferred_element_type=F32)
    return (a[:k] + (a[k:] + b[:k])) + b[k:]


def factor(gram):
    k, lanes = gram.shape
    row = lax.broadcasted_iota(jnp.int32, (k, lanes), 0)
    lane = lax.broadcasted_iota(jnp.int32, (k, lanes), 1)
    a = jnp.where(lane < k, gram, jnp.where(lane - k == row, 1.0, 0.0))
    lower = jnp.zeros((k, lanes), F32)
    scale = jnp.zeros((k, lanes), F32)
    for j in range(k):
        col = jnp.broadcast_to(a[:, j : j + 1], (k, lanes))
        pivot_row = jnp.broadcast_to(a[j : j + 1, :], (k, lanes))
        pivot = jnp.broadcast_to(col[j : j + 1, :], (k, lanes))
        root = lax.rsqrt(pivot)
        a = a - jnp.where(row > j, col * (1.0 / pivot), 0.0) * pivot_row
        lower = jnp.where((lane == j) & (row >= j), col * root, lower)
        scale = jnp.where(row == j, root, scale)
    return lower, a * scale


def columns_of(inverse):
    k, lanes = inverse.shape
    return [jnp.broadcast_to(inverse[:, k + j : k + j + 1], (k, lanes)) for j in range(k)]


def apply(columns, values):
    k, lanes = values.shape
    terms = [columns[j] * jnp.broadcast_to(values[j : j + 1, :], (k, lanes)) for j in range(k)]
    while len(terms) > 1:
        terms = [a + b for a, b in zip(terms[::2], terms[1::2])]
    return terms[0]


def tree_sum(values):
    values = list(values)
    while len(values) > 1:
        pairs = [a + b for a, b in zip(values[::2], values[1::2])]
        if len(values) % 2:
            pairs.append(values[-1])
        values = pairs
    return values[0]


def far_first(n, i):
    return n // 2 + ((i + 1) // 2) * (1 - 2 * (i % 2))


def kernel(
    sizes,
    vec, diag, blocks, rows_in, cols_in, count_in,
    out_x, out_l,
    s_in, s_nn, s_tt, d_in, rows_s, cols_s, count_s,
    x_send, d_send, t_send, g_send,
    rg, cg, cs, rs, gr,
    row_raw, col_in, col_raw, solve,
    in_sem,
    rg_ss, cg_ss, cs_ss, rs_ss, gr_ss,
    rg_rs, cg_rs, cs_rs, rs_rs, gr_rs,
    fr, f_send, f_ss, f_rs,
):
    n_x, n_l, n_k, n_hi, n_lo = sizes
    n_row, n_col = n_x * n_l * n_k, n_hi * n_lo
    slots = blocks.shape[0]
    k, width = x_send.shape
    r = lax.axis_index("row")
    c = lax.axis_index("col")
    hi = c // n_lo
    lo = lax.rem(c, n_lo)
    x = r // (n_l * n_k)
    yl = lax.rem(r // n_k, n_l)
    core = lax.rem(r, n_k)

    def each_row(body):
        inner = n_l * n_k
        tails = [
            lax.rem(yl + far_first(n_l, i // n_k), n_l) * n_k + lax.rem(core + far_first(n_k, i % n_k), n_k)
            for i in range(inner)
        ]

        def outer(a, _):
            base = lax.rem(x + far_first(n_x, a), n_x) * inner
            for i in range(inner):
                body(base + tails[i])
            return 0

        lax.fori_loop(0, n_x - 1, outer, 0)
        for i in range(inner - 1):
            body(x * inner + tails[i])

    bases = [lax.rem(hi + d, n_hi) * n_lo for d in range(n_hi)]
    tails = [lax.rem(lo + d, n_lo) for d in range(n_lo)]
    offsets = [(d, e) for d in range(n_hi) for e in range(n_lo) if (d, e) != (0, 0)]
    offsets.sort(key=lambda o: -(2 * min(o[0], n_hi - o[0]) + min(o[1], n_lo - o[1])))

    def each_col(body):
        for d, e in offsets:
            body(bases[d] + tails[e])

    barrier = pltpu.get_barrier_semaphore()
    each_col(lambda q: pl.semaphore_signal(barrier, inc=1, device_id=(r, q), device_id_type=MESH))
    each_row(lambda q: pl.semaphore_signal(barrier, inc=1, device_id=(q, c), device_id_type=MESH))

    load = [
        pltpu.make_async_copy(blocks, s_in, in_sem.at[0]),
        pltpu.make_async_copy(vec, x_send, in_sem.at[1]),
        pltpu.make_async_copy(diag, d_in, in_sem.at[2]),
        pltpu.make_async_copy(rows_in, rows_s, in_sem.at[3]),
        pltpu.make_async_copy(cols_in, cols_s, in_sem.at[4]),
        pltpu.make_async_copy(count_in, count_s, in_sem.at[5]),
    ]
    for copy in load:
        copy.start()
    for copy in load:
        copy.wait()
    live = count_s[0, 0]
    for b in range(slots):
        keep = jnp.where(b < live, 1.0, 0.0).astype(F32)
        s = s_in[b] * keep
        t = jnp.transpose(s)
        s_hi = s.astype(BF16)
        s_nn[b, :, :width] = s_hi
        s_nn[b, :, width:] = (s - s_hi.astype(F32)).astype(BF16)
        t_hi = t.astype(BF16)
        s_tt[b, :, :width] = t_hi
        s_tt[b, :, width:] = (t - t_hi.astype(F32)).astype(BF16)

    row = lax.broadcasted_iota(jnp.int32, (k, width), 0)
    lane = lax.broadcasted_iota(jnp.int32, (k, width), 1)
    for j in range(k):
        solve[j] = jnp.where(row == j, 1.0, 0.0)
    g_send[...] = jnp.zeros_like(g_send)
    f_send[...] = jnp.zeros_like(f_send)
    pl.semaphore_wait(barrier, n_row + n_col - 2)

    def to_row(q, src, dst, send_sem, recv_sem):
        pltpu.make_async_remote_copy(
            src_ref=src, dst_ref=dst, send_sem=send_sem, recv_sem=recv_sem,
            device_id=(q, c), device_id_type=MESH,
        ).start()

    def to_col(q, src, dst, send_sem, recv_sem):
        pltpu.make_async_remote_copy(
            src_ref=src, dst_ref=dst, send_sem=send_sem, recv_sem=recv_sem,
            device_id=(r, q), device_id_type=MESH,
        ).start()

    def drain(pieces, sem):
        pltpu.make_async_copy(pieces, pieces, sem).wait()

    def gather_row(p):
        each_row(lambda q: to_row(q, x_send, rg.at[p, r], rg_ss, rg_rs.at[p]))

    def gather_col(p):
        each_col(lambda q: to_col(q, x_send, cg.at[p, c], cg_ss, cg_rs.at[p]))

    def solved(pieces):
        terms = [solve[j][None] * pieces[:, j : j + 1, :] for j in range(k)]
        return tree_sum(terms)

    def taken(piece):
        return split_rows(solved(piece[None])[0])

    def take_in(source, p, n, kept):
        for q in range(0, n, 8):
            m = min(8, n - q)
            w = solved(source[p, q : q + m])
            w_hi = w.astype(BF16).astype(F32)
            kept[q : q + m] = jnp.concatenate([w_hi, w - w_hi], axis=1).astype(BF16)

    def gram_kept():
        both = jnp.concatenate([col_in[q] for q in range(n_col)], axis=1)
        dims = (((1,), (1,)), ((), ()))
        a = lax.dot_general(both, both[:k], dims, preferred_element_type=F32)
        b = lax.dot_general(both, both[k:], dims, preferred_element_type=F32)
        return (a[:k] + (a[k:] + b[:k])) + b[k:]

    def pick(parts, place, q):
        return tree_sum(jnp.where(place[b] == q, parts[b], 0.0) for b in range(slots))

    def wait_pieces(buf, p, n, sem):
        drain(buf.at[p, pl.ds(0, n - 1)], sem)

    gather_row(0)
    gather_col(0)
    rg[0, r] = x_send[...]
    cg[0, c] = x_send[...]

    def step(t, _):
        p = lax.rem(t, 2)
        later = 1 - p
        at_row = [rows_s[0, b] for b in range(slots)]
        at_col = [cols_s[0, b] for b in range(slots)]

        wait_pieces(rg, p, n_row, rg_rs.at[p])
        for q in range(n_row):
            row_raw[q] = rg[p, q]
        direct = [product(taken(row_raw[at_col[b]]), s_tt[b]) for b in range(slots)]

        def scatter_col(q):
            d_send[q] = pick(direct, at_row, q)
            to_col(q, d_send.at[q], cs.at[p, c], cs_ss, cs_rs.at[p])

        each_col(scatter_col)
        cs[p, c] = pick(direct, at_row, c)
        own = d_in[...] * tree_sum(solve[j] * x_send[j : j + 1, :] for j in range(k))

        wait_pieces(cg, p, n_col, cg_rs.at[p])
        for q in range(n_col):
            col_raw[q] = cg[p, q]
        trans = [product(taken(col_raw[at_row[b]]), s_nn[b]) for b in range(slots)]

        def scatter_row(q):
            t_send[q] = pick(trans, at_col, q)
            to_row(q, t_send.at[q], rs.at[p, r], rs_ss, rs_rs.at[p])

        each_row(scatter_row)
        rs[p, r] = pick(trans, at_col, r)
        take_in(cg, p, n_col, col_in)
        g_send[:, :k] = gram_kept()
        each_row(lambda q: to_row(q, g_send, gr.at[p, r], gr_ss, gr_rs.at[p]))
        gr[p, r] = g_send[...]

        wait_pieces(rg, p, n_row, rg_ss)
        wait_pieces(cg, p, n_col, cg_ss)
        wait_pieces(cs, p, n_col, cs_rs.at[p])
        own = own + tree_sum(cs[p, i] for i in range(n_col))
        wait_pieces(rs, p, n_row, rs_rs.at[p])
        images = own + tree_sum(rs[p, i] for i in range(n_row))
        x_send[...] = images

        @pl.when(t < ITERS - 1)
        def _():
            gather_row(later)

        gather_col(later)
        rg[later, r] = images
        cg[later, c] = images

        wait_pieces(gr, p, n_row, gr_rs.at[p])
        gram = tree_sum(gr[p, i] for i in range(n_row))
        gram = jnp.where(t == 0, jnp.where(row == lane, 1.0, 0.0), gram)
        columns = columns_of(factor(gram)[1])
        for j in range(k):
            solve[j] = columns[j]
        wait_pieces(cs, p, n_col, cs_ss)
        wait_pieces(rs, p, n_row, rs_ss)
        wait_pieces(gr, p, n_row, gr_ss)
        return 0

    lax.fori_loop(0, ITERS, step, 0)

    last = ITERS % 2
    wait_pieces(cg, last, n_col, cg_rs.at[last])
    take_in(cg, last, n_col, col_in)
    f_send[:, :k] = gram_kept()
    each_row(lambda q: to_row(q, f_send, fr.at[r], f_ss, f_rs))
    fr[r] = f_send[...]
    images = tree_sum(solve[j] * x_send[j : j + 1, :] for j in range(k))
    drain(fr.at[pl.ds(0, n_row - 1)], f_rs)
    lower, inverse = factor(tree_sum(fr[i] for i in range(n_row)))
    out_x[...] = apply(columns_of(inverse), images)
    out_l[...] = lower[:, :k]
    wait_pieces(cg, last, n_col, cg_ss)
    drain(fr.at[pl.ds(0, n_row - 1)], f_ss)


def solution(mesh):
    n_row, n_col = mesh.shape["row"], mesh.shape["col"]
    n_k = 2 if n_row % 2 == 0 else 1
    n_l = 2 if n_row % 4 == 0 else 1
    n_x = n_row // (n_k * n_l)
    n_hi = 4 if n_col % 8 == 0 else 2
    n_lo = n_col // n_hi

    def shards(vectors, diagonal, blocks, block_rows, block_cols, counts):
        k, width = vectors.shape
        slots = blocks.shape[2]
        piece = (k, width)
        vmem = pl.BlockSpec(memory_space=pltpu.VMEM)
        left = pl.BlockSpec(memory_space=pl.ANY)
        dma = pltpu.SemaphoreType.DMA
        return pl.pallas_call(
            functools.partial(kernel, (n_x, n_l, n_k, n_hi, n_lo)),
            out_shape=(pltpu.VMEM(piece, F32), pltpu.VMEM((k, k), F32)),
            in_specs=[left] * 6,
            out_specs=(vmem, vmem),
            scratch_shapes=[
                pltpu.VMEM((slots, width, width), F32),
                pltpu.VMEM((slots, width, 2 * width), BF16),
                pltpu.VMEM((slots, width, 2 * width), BF16),
                pltpu.VMEM((1, width), F32),
                pltpu.SMEM((1, slots), jnp.int32),
                pltpu.SMEM((1, slots), jnp.int32),
                pltpu.SMEM((1, 1), jnp.int32),
                pltpu.VMEM(piece, F32),
                pltpu.VMEM((n_col,) + piece, F32),
                pltpu.VMEM((n_row,) + piece, F32),
                pltpu.VMEM(piece, F32),
                pltpu.VMEM((2, n_row) + piece, F32),
                pltpu.VMEM((2, n_col) + piece, F32),
                pltpu.VMEM((2, n_col) + piece, F32),
                pltpu.VMEM((2, n_row) + piece, F32),
                pltpu.VMEM((2, n_row) + piece, F32),
                pltpu.VMEM((n_row,) + piece, F32),
                pltpu.VMEM((n_col, 2 * k, width), BF16),
                pltpu.VMEM((n_col,) + piece, F32),
                pltpu.VMEM((k,) + piece, F32),
                dma((6,)),
                dma, dma, dma, dma, dma,
                dma((2,)), dma((2,)), dma((2,)), dma((2,)), dma((2,)),
                pltpu.VMEM((n_row,) + piece, F32),
                pltpu.VMEM(piece, F32),
                dma,
                dma,
            ],
            compiler_params=pltpu.CompilerParams(
                collective_id=0, has_side_effects=True, vmem_limit_bytes=60 * 1024 * 1024
            ),
        )(
            vectors, diagonal.reshape(1, width), blocks.reshape(slots, width, width),
            block_rows.reshape(1, slots), block_cols.reshape(1, slots), counts,
        )

    return jax.shard_map(
        shards,
        mesh=mesh,
        in_specs=(
            P(None, ("row", "col")),
            P(("row", "col")),
            P("row", "col", None, None, None),
            P("row", "col", None),
            P("row", "col", None),
            P("row", "col"),
        ),
        out_specs=(P(None, ("row", "col")), P()),
        check_vma=False,
    )
```

```python
import functools

import jax
import jax.numpy as jnp
from jax import lax
from jax.experimental import pallas as pl
from jax.experimental.pallas import tpu as pltpu
from jax.sharding import PartitionSpec as P

ITERS = 4
MESH = pl.DeviceIdType.MESH
F32 = jnp.float32
BF16 = jnp.bfloat16


def split_rows(x):
    hi = x.astype(BF16).astype(F32)
    return jnp.concatenate([hi, x - hi], axis=0).astype(BF16)


def product(both, pair):
    out = jnp.dot(both, pair, preferred_element_type=F32)
    k = both.shape[0] // 2
    n = pair.shape[1] // 2
    return (out[:k, :n] + (out[k:, :n] + out[:k, n:])) + out[k:, n:]


def gram_of(wide):
    both = split_rows(wide)
    k = wide.shape[0]
    dims = (((1,), (1,)), ((), ()))
    high = both[:k]
    low = both[k:]
    a = lax.dot_general(both, high, dims, preferred_element_type=F32)
    b = lax.dot_general(both, low, dims, preferred_element_type=F32)
    return (a[:k] + (a[k:] + b[:k])) + b[k:]


def factor(gram):
    k, lanes = gram.shape
    row = lax.broadcasted_iota(jnp.int32, (k, lanes), 0)
    lane = lax.broadcasted_iota(jnp.int32, (k, lanes), 1)
    a = jnp.where(lane < k, gram, jnp.where(lane - k == row, 1.0, 0.0))
    lower = jnp.zeros((k, lanes), F32)
    scale = jnp.zeros((k, lanes), F32)
    for j in range(0, k, 2):
        col = jnp.broadcast_to(a[:, j : j + 1], (k, lanes))
        col_b = jnp.broadcast_to(a[:, j + 1 : j + 2], (k, lanes))
        line = jnp.broadcast_to(a[j : j + 1, :], (k, lanes))
        line_b = jnp.broadcast_to(a[j + 1 : j + 2, :], (k, lanes))
        pivot = jnp.broadcast_to(col[j : j + 1, :], (k, lanes))
        beside = jnp.broadcast_to(col[j + 1 : j + 2, :], (k, lanes))
        pivot_b = jnp.broadcast_to(col_b[j + 1 : j + 2, :], (k, lanes))
        inverse = 1.0 / pivot
        ratio = beside * inverse
        pivot_b = pivot_b - ratio * beside
        line_b = line_b - ratio * line
        col_b = col_b - ratio * col
        a = (a - jnp.where(row > j, col * inverse, 0.0) * line) - jnp.where(row > j + 1, col_b * (1.0 / pivot_b), 0.0) * line_b
        root = lax.rsqrt(pivot)
        root_b = lax.rsqrt(pivot_b)
        lower = jnp.where((lane == j) & (row >= j), col * root, lower)
        lower = jnp.where((lane == j + 1) & (row >= j + 1), col_b * root_b, lower)
        scale = jnp.where(row == j, root, jnp.where(row == j + 1, root_b, scale))
    return lower, a * scale


def columns_of(inverse):
    k, lanes = inverse.shape
    return [jnp.broadcast_to(inverse[:, k + j : k + j + 1], (k, lanes)) for j in range(k)]


def apply(columns, values):
    k, lanes = values.shape
    terms = [columns[j] * jnp.broadcast_to(values[j : j + 1, :], (k, lanes)) for j in range(k)]
    while len(terms) > 1:
        terms = [a + b for a, b in zip(terms[::2], terms[1::2])]
    return terms[0]


def tree_sum(values):
    values = list(values)
    while len(values) > 1:
        pairs = [a + b for a, b in zip(values[::2], values[1::2])]
        if len(values) % 2:
            pairs.append(values[-1])
        values = pairs
    return values[0]


def far_first(n, i):
    return n // 2 + ((i + 1) // 2) * (1 - 2 * (i % 2))


def kernel(
    sizes,
    vec, diag, blocks, rows_in, cols_in, count_in,
    out_x, out_l,
    s_in, s_nn, s_tt, d_in, rows_s, cols_s, count_s,
    x_send, d_send, t_send, g_send,
    rg, cg, cs, rs, gr,
    row_raw, col_in, col_raw, solve,
    in_sem,
    rg_ss, cg_ss, cs_ss, rs_ss, gr_ss,
    rg_rs, cg_rs, cs_rs, rs_rs, gr_rs,
    fr, f_send, f_ss, f_rs,
):
    n_x, n_l, n_k, n_hi, n_lo = sizes
    n_row, n_col = n_x * n_l * n_k, n_hi * n_lo
    slots = blocks.shape[0]
    k, width = x_send.shape
    r = lax.axis_index("row")
    c = lax.axis_index("col")
    hi = c // n_lo
    lo = lax.rem(c, n_lo)
    x = r // (n_l * n_k)
    yl = lax.rem(r // n_k, n_l)
    core = lax.rem(r, n_k)

    def each_row(body):
        inner = n_l * n_k
        tails = [
            lax.rem(yl + far_first(n_l, i // n_k), n_l) * n_k + lax.rem(core + far_first(n_k, i % n_k), n_k)
            for i in range(inner)
        ]

        def outer(a, _):
            base = lax.rem(x + far_first(n_x, a), n_x) * inner
            for i in range(inner):
                body(base + tails[i])
            return 0

        lax.fori_loop(0, n_x - 1, outer, 0)
        for i in range(inner - 1):
            body(x * inner + tails[i])

    bases = [lax.rem(hi + d, n_hi) * n_lo for d in range(n_hi)]
    tails = [lax.rem(lo + d, n_lo) for d in range(n_lo)]
    offsets = [(d, e) for d in range(n_hi) for e in range(n_lo) if (d, e) != (0, 0)]
    offsets.sort(key=lambda o: -(2 * min(o[0], n_hi - o[0]) + min(o[1], n_lo - o[1])))

    def each_col(body):
        for d, e in offsets:
            body(bases[d] + tails[e])

    barrier = pltpu.get_barrier_semaphore()
    each_col(lambda q: pl.semaphore_signal(barrier, inc=1, device_id=(r, q), device_id_type=MESH))
    each_row(lambda q: pl.semaphore_signal(barrier, inc=1, device_id=(q, c), device_id_type=MESH))

    load = [
        pltpu.make_async_copy(blocks, s_in, in_sem.at[0]),
        pltpu.make_async_copy(vec, x_send, in_sem.at[1]),
        pltpu.make_async_copy(diag, d_in, in_sem.at[2]),
        pltpu.make_async_copy(rows_in, rows_s, in_sem.at[3]),
        pltpu.make_async_copy(cols_in, cols_s, in_sem.at[4]),
        pltpu.make_async_copy(count_in, count_s, in_sem.at[5]),
    ]
    for copy in load:
        copy.start()
    for copy in load:
        copy.wait()
    live = count_s[0, 0]
    for b in range(slots):
        keep = jnp.where(b < live, 1.0, 0.0).astype(F32)
        s = s_in[b] * keep
        t = jnp.transpose(s)
        s_hi = s.astype(BF16)
        s_nn[b, :, :width] = s_hi
        s_nn[b, :, width:] = (s - s_hi.astype(F32)).astype(BF16)
        t_hi = t.astype(BF16)
        s_tt[b, :, :width] = t_hi
        s_tt[b, :, width:] = (t - t_hi.astype(F32)).astype(BF16)

    row = lax.broadcasted_iota(jnp.int32, (k, width), 0)
    lane = lax.broadcasted_iota(jnp.int32, (k, width), 1)
    for j in range(k):
        solve[j] = jnp.where(row == j, 1.0, 0.0)
    g_send[...] = jnp.zeros_like(g_send)
    f_send[...] = jnp.zeros_like(f_send)
    pl.semaphore_wait(barrier, n_row + n_col - 2)

    def to_row(q, src, dst, send_sem, recv_sem):
        pltpu.make_async_remote_copy(
            src_ref=src, dst_ref=dst, send_sem=send_sem, recv_sem=recv_sem,
            device_id=(q, c), device_id_type=MESH,
        ).start()

    def to_col(q, src, dst, send_sem, recv_sem):
        pltpu.make_async_remote_copy(
            src_ref=src, dst_ref=dst, send_sem=send_sem, recv_sem=recv_sem,
            device_id=(r, q), device_id_type=MESH,
        ).start()

    def drain(pieces, sem):
        pltpu.make_async_copy(pieces, pieces, sem).wait()

    def gather_row(p):
        each_row(lambda q: to_row(q, x_send, rg.at[p, r], rg_ss, rg_rs.at[p]))

    def gather_col(p):
        each_col(lambda q: to_col(q, x_send, cg.at[p, c], cg_ss, cg_rs.at[p]))

    def solved(pieces):
        terms = [solve[j][None] * pieces[:, j : j + 1, :] for j in range(k)]
        return tree_sum(terms)

    def taken(piece):
        return split_rows(solved(piece[None])[0])

    def take_in(source, p, n, kept):
        for q in range(0, n, 8):
            m = min(8, n - q)
            w = solved(source[p, q : q + m])
            w_hi = w.astype(BF16).astype(F32)
            kept[q : q + m] = jnp.concatenate([w_hi, w - w_hi], axis=1).astype(BF16)

    def gram_kept(n):
        both = jnp.concatenate([col_in[q] for q in range(n)], axis=1)
        dims = (((1,), (1,)), ((), ()))
        a = lax.dot_general(both, both[:k], dims, preferred_element_type=F32)
        b = lax.dot_general(both, both[k:], dims, preferred_element_type=F32)
        return (a[:k] + (a[k:] + b[:k])) + b[k:]

    def pick(parts, place, q):
        return tree_sum(jnp.where(place[b] == q, parts[b], 0.0) for b in range(slots))

    def wait_pieces(buf, p, n, sem):
        drain(buf.at[p, pl.ds(0, n - 1)], sem)

    gather_row(0)
    gather_col(0)
    rg[0, r] = x_send[...]
    cg[0, c] = x_send[...]

    def step(t, _):
        p = lax.rem(t, 2)
        later = 1 - p
        at_row = [rows_s[0, b] for b in range(slots)]
        at_col = [cols_s[0, b] for b in range(slots)]

        wait_pieces(rg, p, n_row, rg_rs.at[p])
        for q in range(n_row):
            row_raw[q] = rg[p, q]
        direct = [product(taken(row_raw[at_col[b]]), s_tt[b]) for b in range(slots)]

        def scatter_col(q):
            d_send[q] = pick(direct, at_row, q)
            to_col(q, d_send.at[q], cs.at[p, c], cs_ss, cs_rs.at[p])

        each_col(scatter_col)
        cs[p, c] = pick(direct, at_row, c)
        own = d_in[...] * tree_sum(solve[j] * x_send[j : j + 1, :] for j in range(k))

        wait_pieces(cg, p, n_col, cg_rs.at[p])
        for q in range(n_col):
            col_raw[q] = cg[p, q]
        trans = [product(taken(col_raw[at_row[b]]), s_nn[b]) for b in range(slots)]

        def scatter_row(q):
            t_send[q] = pick(trans, at_col, q)
            to_row(q, t_send.at[q], rs.at[p, r], rs_ss, rs_rs.at[p])

        each_row(scatter_row)
        rs[p, r] = pick(trans, at_col, r)
        take_in(cg, p, n_col, col_in)
        g_send[:, :k] = gram_kept(n_col)
        each_row(lambda q: to_row(q, g_send, gr.at[p, r], gr_ss, gr_rs.at[p]))
        gr[p, r] = g_send[...]

        wait_pieces(rg, p, n_row, rg_ss)
        wait_pieces(cg, p, n_col, cg_ss)
        wait_pieces(cs, p, n_col, cs_rs.at[p])
        own = own + tree_sum(cs[p, i] for i in range(n_col))
        wait_pieces(rs, p, n_row, rs_rs.at[p])
        images = own + tree_sum(rs[p, i] for i in range(n_row))
        x_send[...] = images

        gather_row(later)

        @pl.when(t < ITERS - 1)
        def _():
            gather_col(later)

        rg[later, r] = images
        cg[later, c] = images

        wait_pieces(gr, p, n_row, gr_rs.at[p])
        gram = tree_sum(gr[p, i] for i in range(n_row))
        gram = jnp.where(t == 0, jnp.where(row == lane, 1.0, 0.0), gram)
        columns = columns_of(factor(gram)[1])
        for j in range(k):
            solve[j] = columns[j]
        wait_pieces(cs, p, n_col, cs_ss)
        wait_pieces(rs, p, n_row, rs_ss)
        wait_pieces(gr, p, n_row, gr_ss)
        return 0

    lax.fori_loop(0, ITERS, step, 0)

    last = ITERS % 2
    wait_pieces(rg, last, n_row, rg_rs.at[last])
    take_in(rg, last, n_row, col_in)
    f_send[:, :k] = gram_kept(n_row)
    each_col(lambda q: to_col(q, f_send, fr.at[c], f_ss, f_rs))
    fr[c] = f_send[...]
    images = tree_sum(solve[j] * x_send[j : j + 1, :] for j in range(k))
    drain(fr.at[pl.ds(0, n_col - 1)], f_rs)
    lower, inverse = factor(tree_sum(fr[i] for i in range(n_col)))
    out_x[...] = apply(columns_of(inverse), images)
    out_l[...] = lower[:, :k]
    wait_pieces(rg, last, n_row, rg_ss)
    drain(fr.at[pl.ds(0, n_col - 1)], f_ss)


def solution(mesh):
    n_row, n_col = mesh.shape["row"], mesh.shape["col"]
    n_k = 2 if n_row % 2 == 0 else 1
    n_l = 2 if n_row % 4 == 0 else 1
    n_x = n_row // (n_k * n_l)
    n_hi = 4 if n_col % 8 == 0 else 2
    n_lo = n_col // n_hi

    def shards(vectors, diagonal, blocks, block_rows, block_cols, counts):
        k, width = vectors.shape
        slots = blocks.shape[2]
        piece = (k, width)
        vmem = pl.BlockSpec(memory_space=pltpu.VMEM)
        left = pl.BlockSpec(memory_space=pl.ANY)
        dma = pltpu.SemaphoreType.DMA
        return pl.pallas_call(
            functools.partial(kernel, (n_x, n_l, n_k, n_hi, n_lo)),
            out_shape=(pltpu.VMEM(piece, F32), pltpu.VMEM((k, k), F32)),
            in_specs=[left] * 6,
            out_specs=(vmem, vmem),
            scratch_shapes=[
                pltpu.VMEM((slots, width, width), F32),
                pltpu.VMEM((slots, width, 2 * width), BF16),
                pltpu.VMEM((slots, width, 2 * width), BF16),
                pltpu.VMEM((1, width), F32),
                pltpu.SMEM((1, slots), jnp.int32),
                pltpu.SMEM((1, slots), jnp.int32),
                pltpu.SMEM((1, 1), jnp.int32),
                pltpu.VMEM(piece, F32),
                pltpu.VMEM((n_col,) + piece, F32),
                pltpu.VMEM((n_row,) + piece, F32),
                pltpu.VMEM(piece, F32),
                pltpu.VMEM((2, n_row) + piece, F32),
                pltpu.VMEM((2, n_col) + piece, F32),
                pltpu.VMEM((2, n_col) + piece, F32),
                pltpu.VMEM((2, n_row) + piece, F32),
                pltpu.VMEM((2, n_row) + piece, F32),
                pltpu.VMEM((n_row,) + piece, F32),
                pltpu.VMEM((n_col, 2 * k, width), BF16),
                pltpu.VMEM((n_col,) + piece, F32),
                pltpu.VMEM((k,) + piece, F32),
                dma((6,)),
                dma, dma, dma, dma, dma,
                dma((2,)), dma((2,)), dma((2,)), dma((2,)), dma((2,)),
                pltpu.VMEM((n_col,) + piece, F32),
                pltpu.VMEM(piece, F32),
                dma,
                dma,
            ],
            compiler_params=pltpu.CompilerParams(
                collective_id=0, has_side_effects=True, vmem_limit_bytes=60 * 1024 * 1024
            ),
        )(
            vectors, diagonal.reshape(1, width), blocks.reshape(slots, width, width),
            block_rows.reshape(1, slots), block_cols.reshape(1, slots), counts,
        )

    return jax.shard_map(
        shards,
        mesh=mesh,
        in_specs=(
            P(None, ("row", "col")),
            P(("row", "col")),
            P("row", "col", None, None, None),
            P("row", "col", None),
            P("row", "col", None),
            P("row", "col"),
        ),
        out_specs=(P(None, ("row", "col")), P()),
        check_vma=False,
    )
```
